32 devices in a mesh: rep: 8 (over y, x, core), shard: 4 (over z).
Axes of the slice: x: 2, y: 2, z: 4, core: 2. Of those that a mesh axis runs over, the one named last changes fastest.
Arguments:
- tokens: bfloat16 [8192, 2048], P(('rep', 'shard')), may hold values from -6 to 6
- cotangent: bfloat16 [8192, 2048], P(('rep', 'shard')), may hold values from -6 to 6
- segment_ids: int32 [8192], P('rep'), may hold values from 0 to 4, as said below
- positions: int32 [8192], P(('rep', 'shard')), may hold values from 0 to 958, as said below
- projection_weight: float32 [2048, 3072], P(('shard', 'rep')), may hold values from -0.125 to 0.125
- projection_first_moment: float32 [2048, 3072], P(('shard', 'rep')), may hold values from -32 to 32
- projection_second_moment: float32 [2048, 3072], P(('shard', 'rep')), may hold values from 53.894737 to 431.1579
- out_weight: float32 [2048, 2048], P(None, ('shard', 'rep')), may hold values from -1 to 1
- out_first: float32 [2048, 2048], P(None, ('shard', 'rep')), may hold values from -6 to 6
- out_second: float32 [2048, 2048], P(None, ('shard', 'rep')), may hold values from 1.8947369 to 15.157895
- gate_up_weight: float32 [2048, 16384], P(('shard', 'rep')), may hold values from -0.125 to 0.125
- gate_up_first: float32 [2048, 16384], P(('shard', 'rep')), may hold values from -32 to 32
- gate_up_second: float32 [2048, 16384], P(('shard', 'rep')), may hold values from 53.894737 to 431.1579
- down_weight: float32 [8192, 2048], P(None, ('shard', 'rep')), may hold values from -0.0625 to 0.0625
- down_first: float32 [8192, 2048], P(None, ('shard', 'rep')), may hold values from -32 to 32
- down_second: float32 [8192, 2048], P(None, ('shard', 'rep')), may hold values from 77.60842 to 620.8674
- norm_gains: float32 [2, 2048], P(None, ('shard', 'rep')), may hold values from 0.5 to 1.5
- gains_first: float32 [2, 2048], P(None, ('shard', 'rep')), may hold values from -64 to 64
- gains_second: float32 [2, 2048], P(None, ('shard', 'rep')), may hold values from 215.57895 to 1724.6316
Outputs:
- layer_out: bfloat16 [8192, 2048], P(('rep', 'shard'))
- tokens_grad: bfloat16 [8192, 2048], P(('rep', 'shard'))
- qkv_first_new: float32 [2048, 3072], P(('shard', 'rep'))
- qkv_second_new: float32 [2048, 3072], P(('shard', 'rep'))
- qkv_weight_new: float32 [2048, 3072], P(('shard', 'rep'))
- out_first_new: float32 [2048, 2048], P(None, ('shard', 'rep'))
- out_second_new: float32 [2048, 2048], P(None, ('shard', 'rep'))
- out_weight_new: float32 [2048, 2048], P(None, ('shard', 'rep'))
- gate_up_first_new: float32 [2048, 16384], P(('shard', 'rep'))
- gate_up_second_new: float32 [2048, 16384], P(('shard', 'rep'))
- gate_up_weight_new: float32 [2048, 16384], P(('shard', 'rep'))
- down_first_new: float32 [8192, 2048], P(None, ('shard', 'rep'))
- down_second_new: float32 [8192, 2048], P(None, ('shard', 'rep'))
- down_weight_new: float32 [8192, 2048], P(None, ('shard', 'rep'))
- gains_first_new: float32 [2, 2048], P(None, ('shard', 'rep'))
- gains_second_new: float32 [2, 2048], P(None, ('shard', 'rep'))
- gains_new: float32 [2, 2048], P(None, ('shard', 'rep'))
The draws below stay inside these ranges and needn't reach their ends.
Inputs may be any that keep to these rules, and one draw needn't show every extreme that they name: `segment_ids`: within each group of 1024 rows the segment numbers never fall, so segments are runs of consecutive rows; one segment of each group starts in the rows of the group's first device and ends in those of its last. `positions`: positions count up by one from 0 along each segment; the longest segment of each group has 959 rows.
All inputs are finite; a program needn't handle non-finite values.
Results may differ from the reference program's by a relative error of at most 0.025.
Values may be sent and summed in bfloat16 or wider, within the bound.
A program may use at most 1 GiB of HBM per device.

```python
import math
import jax
import jax.numpy as jnp
from jax import lax

MODEL_WIDTH = 2048
QUERY_HEADS = 32
KEY_VALUE_HEADS = 8
HEAD_SIZE = 64
FF = 8192
TOK_DEV = 256
STEP = 5
GROUP_TOKENS = 1024
TOKEN_TOTAL = 8192


def segment_layout(key):
    key = jax.random.fold_in(key, 101)
    key_a, key_c, key_d = jax.random.split(key, 3)
    num_groups = TOKEN_TOTAL // GROUP_TOKENS
    reach = TOK_DEV // 4 + 1
    head_len = jax.random.randint(key_a, (num_groups, 1), 1, reach)
    tail_len = reach - head_len
    first_cut = jnp.minimum(jax.random.randint(key_c, (num_groups, 1), 1, reach), head_len)
    long_end = GROUP_TOKENS - tail_len
    last_cut = long_end + jnp.minimum(jax.random.randint(key_d, (num_groups, 1), 0, reach), tail_len - 1)
    row_index = jnp.arange(GROUP_TOKENS, dtype=jnp.int32)[None, :]
    seg_rows = jnp.zeros((num_groups, GROUP_TOKENS), jnp.int32)
    start_rows = jnp.zeros((num_groups, GROUP_TOKENS), jnp.int32)
    for cut_at in (first_cut, head_len, long_end, last_cut):
        passed = row_index >= cut_at
        seg_rows = seg_rows + passed.astype(jnp.int32)
        start_rows = jnp.maximum(start_rows, jnp.where(passed, cut_at, 0))
    return (seg_rows.reshape(-1), (row_index - start_rows).reshape(-1))


def draw_segment_ids(key, part):
    seg_rows, pos_rows = segment_layout(key)
    return seg_rows


def draw_positions(key, part):
    seg_rows, pos_rows = segment_layout(key)
    return pos_rows


def strengthened(values, key, source, target, shards_of, factor):
    owner, partner = [(jnp.arange(values.shape[axis_at]) // (values.shape[axis_at] // shards_of)).reshape([-1 if axis == axis_at else 1 for axis in range(values.ndim)]) for axis_at in (source, target)]
    chosen = jax.random.permutation(key, shards_of)[partner]
    strong = (owner == chosen) | (owner == (partner + shards_of // 2) % shards_of)
    return jnp.where(strong, factor * values, values)


def level_of(rng, dims, cuts, smallest, top_value):
    gain, own = 1.0, jax.random.fold_in(rng, 6)
    for axis_at, shards_of in cuts:
        steps = jnp.exp(jax.random.uniform(jax.random.fold_in(own, axis_at), (shards_of,), jnp.float32, smallest / len(cuts), top_value / len(cuts)))
        gain = gain * jnp.repeat(steps, dims[axis_at] // shards_of).reshape([-1 if axis == axis_at else 1 for axis in range(len(dims))])
    return gain


def bell_draw(rng, shape, deviation, limit, pieces=(), kind=jnp.bfloat16):
    factor_of = level_of(rng, shape, pieces, -0.22, 0.18) if pieces else 1.0
    drawn = jax.random.normal(rng, shape, jnp.float32) * deviation * factor_of
    return jnp.minimum(jnp.maximum(drawn, -limit), limit).astype(kind)


def gaussian_with(rng, extent, spread, bound, shards, heavy, kind=jnp.bfloat16):
    drawn = spread * jax.random.normal(rng, extent, jnp.float32)
    if shards:
        drawn = drawn * level_of(rng, extent, shards, -0.22, 0.18)
    return jnp.clip(strengthened(drawn, jax.random.fold_in(rng, 3), *heavy), -bound, bound).astype(kind)


def setup_inputs(seed: int = 0) -> dict:
    arg_keys = jax.random.split(jax.random.key(seed), 20)
    tokens = gaussian_with(arg_keys[0], (TOKEN_TOTAL, MODEL_WIDTH), 1.0, 6.0, ((0, 32),), (0, 1, 32, 2.75))
    cotangent = bell_draw(arg_keys[1], (TOKEN_TOTAL, MODEL_WIDTH), 1.0, 6.0, ((0, 32),))
    segment_ids = draw_segment_ids(jax.random.fold_in(arg_keys[19], 71), 0)
    positions = draw_positions(jax.random.fold_in(arg_keys[19], 71), 0)
    projection_weight = bell_draw(arg_keys[4], (MODEL_WIDTH, (QUERY_HEADS + 2 * KEY_VALUE_HEADS) * HEAD_SIZE), MODEL_WIDTH ** -0.5, 0.125, ((0, 32),), jnp.float32)
    projection_first_moment = bell_draw(arg_keys[5], (MODEL_WIDTH, (QUERY_HEADS + 2 * KEY_VALUE_HEADS) * HEAD_SIZE), (16 * (TOKEN_TOTAL // GROUP_TOKENS) ** 0.5 / 9), 32.0, ((0, 32),), jnp.float32)
    projection_second_moment = jnp.clip(jnp.exp(math.log(431.1579) - 2.0794415 * jax.random.uniform(arg_keys[6], (MODEL_WIDTH, (QUERY_HEADS + 2 * KEY_VALUE_HEADS) * HEAD_SIZE), jnp.float32) ** level_of(arg_keys[6], (MODEL_WIDTH, (QUERY_HEADS + 2 * KEY_VALUE_HEADS) * HEAD_SIZE), ((0, 32),), -0.2, 0.2)), 53.894737, 431.1579)
    out_weight = bell_draw(arg_keys[7], (QUERY_HEADS * HEAD_SIZE, MODEL_WIDTH), 32 ** -0.5, 1.0, ((1, 32),), jnp.float32)
    out_first = bell_draw(arg_keys[8], (QUERY_HEADS * HEAD_SIZE, MODEL_WIDTH), (3 * (TOKEN_TOTAL // GROUP_TOKENS) ** 0.5 / 9), 6.0, ((1, 32),), jnp.float32)
    out_second = jnp.clip(jnp.exp(math.log(15.157895) - 2.0794415 * jax.random.uniform(arg_keys[9], (QUERY_HEADS * HEAD_SIZE, MODEL_WIDTH), jnp.float32) ** level_of(arg_keys[9], (QUERY_HEADS * HEAD_SIZE, MODEL_WIDTH), ((1, 32),), -0.2, 0.2)), 1.8947369, 15.157895)
    gate_up_weight = bell_draw(arg_keys[10], (MODEL_WIDTH, 2 * FF), MODEL_WIDTH ** -0.5, 0.125, ((0, 32),), jnp.float32)
    gate_up_first = bell_draw(arg_keys[11], (MODEL_WIDTH, 2 * FF), (0.5 * TOKEN_TOTAL ** 0.5 / 9), 32.0, ((0, 32),), jnp.float32)
    gate_up_second = jnp.clip(jnp.exp(math.log(431.1579) - 2.0794415 * jax.random.uniform(arg_keys[12], (MODEL_WIDTH, 2 * FF), jnp.float32) ** level_of(arg_keys[12], (MODEL_WIDTH, 2 * FF), ((0, 32),), -0.2, 0.2)), 53.894737, 431.1579)
    down_weight = bell_draw(arg_keys[13], (FF, MODEL_WIDTH), FF ** -0.5, 0.0625, ((1, 32),), jnp.float32)
    down_first = bell_draw(arg_keys[14], (FF, MODEL_WIDTH), (0.6 * TOKEN_TOTAL ** 0.5 / 9), 32.0, ((1, 32),), jnp.float32)
    down_second = jnp.clip(jnp.exp(math.log(620.8674) - 2.0794415 * jax.random.uniform(arg_keys[15], (FF, MODEL_WIDTH), jnp.float32) ** level_of(arg_keys[15], (FF, MODEL_WIDTH), ((1, 32),), -0.2, 0.2)), 77.60842, 620.8674)
    norm_gains = jnp.clip(1.0 + 0.1 * jax.random.normal(arg_keys[16], (2, MODEL_WIDTH), jnp.float32), 0.5, 1.5)
    gains_first = bell_draw(arg_keys[17], (2, MODEL_WIDTH), (TOKEN_TOTAL ** 0.5 / 9), 64.0, ((1, 32),), jnp.float32)
    gains_second = jnp.clip(jnp.exp(math.log(1724.6316) - 2.0794415 * jax.random.uniform(arg_keys[18], (2, MODEL_WIDTH), jnp.float32) ** level_of(arg_keys[18], (2, MODEL_WIDTH), ((1, 32),), -0.2, 0.2)), 215.57895, 1724.6316)
    return {"tokens": tokens, "cotangent": cotangent, "segment_ids": segment_ids, "positions": positions, "projection_weight": projection_weight, "projection_first_moment": projection_first_moment, "projection_second_moment": projection_second_moment, "out_weight": out_weight, "out_first": out_first, "out_second": out_second, "gate_up_weight": gate_up_weight, "gate_up_first": gate_up_first, "gate_up_second": gate_up_second, "down_weight": down_weight, "down_first": down_first, "down_second": down_second, "norm_gains": norm_gains, "gains_first": gains_first, "gains_second": gains_second}


@jax.custom_vjp
def low(v):
    return lax.optimization_barrier(v.astype(jnp.bfloat16)).astype(jnp.float32)

@jax.custom_vjp
def low_back(v):
    return v

def low_keep(v):
    return (low(v), None)

def low_pass(kept, grad):
    return (grad,)

def back_keep(v):
    return (v, None)

def back_low(kept, grad):
    return (low(grad),)
low.defvjp(low_keep, low_pass)
low_back.defvjp(back_keep, back_low)
RATES = (0.05, 0.4, 0.05, 0.03, 1.0)
DECAYS = (0.1, 0.1, 0.1, 0.1, 0.0)

def matmul_hi(left, right):
    return jnp.dot(left, right, precision=lax.Precision.HIGHEST, preferred_element_type=jnp.float32)

def rms_scale(value):
    return lax.rsqrt(lax.optimization_barrier(jnp.mean(value * value, axis=-1, keepdims=True)) + 1e-05)

def angles(position_rows):
    freq = 500000.0 ** (-jnp.arange(HEAD_SIZE // 2, dtype=jnp.float32) * 2.0 / HEAD_SIZE)
    phase = position_rows.astype(jnp.float32)[:, None] * freq[None, :]
    phase = jnp.concatenate([phase, phase], axis=-1)
    return (jnp.cos(phase), jnp.sin(phase))

def rotate(flat, cos_table, sin_table):
    num_rows = flat.shape[0]
    half_dim = HEAD_SIZE // 2
    heads = flat.reshape(num_rows, -1, HEAD_SIZE)
    turned = jnp.concatenate([-heads[..., half_dim:], heads[..., :half_dim]], axis=-1)
    return (heads * cos_table[:, None, :] + turned * sin_table[:, None, :]).reshape(num_rows, -1)

def attend_block(query_rows, query_seg, query_index, key_row_block, value_row_block, key_seg):
    rows_of_block = query_rows.shape[0]
    grouped_heads = query_rows.reshape(rows_of_block, KEY_VALUE_HEADS, QUERY_HEADS // KEY_VALUE_HEADS, HEAD_SIZE)
    key_head_split = key_row_block.reshape(-1, KEY_VALUE_HEADS, HEAD_SIZE)
    value_head_split = value_row_block.reshape(-1, KEY_VALUE_HEADS, HEAD_SIZE)
    scores = jnp.einsum('qhgd,khd->hgqk', grouped_heads, key_head_split, precision=lax.Precision.HIGHEST) * HEAD_SIZE ** (-0.5)
    scores = low_back(scores)
    key_index = jnp.arange(key_row_block.shape[0], dtype=jnp.int32)
    allowed = (query_seg[:, None] == key_seg[None, :]) & (key_index[None, :] <= query_index[:, None])
    scores = jnp.where(allowed[None, None], scores, -1e+30)
    peak_score = lax.optimization_barrier(jnp.max(scores, axis=-1, keepdims=True))
    expd = jnp.exp(scores - peak_score)
    probs = low(expd / lax.optimization_barrier(jnp.sum(expd, axis=-1, keepdims=True)))
    attended = jnp.einsum('hgqk,khd->qhgd', probs, value_head_split, precision=lax.Precision.HIGHEST)
    return attended.reshape(rows_of_block, QUERY_HEADS * HEAD_SIZE)

def layer_forward(params, tokens_f, seg_rows, cos_table, sin_table):
    w_qkv, w_out, w_gu, w_down, gain_rows = params
    q_width = QUERY_HEADS * HEAD_SIZE
    key_value_width = KEY_VALUE_HEADS * HEAD_SIZE
    normed_one = low(tokens_f * rms_scale(tokens_f) * gain_rows[0])
    qkv_proj = low_back(matmul_hi(normed_one, w_qkv))
    query_rows = low(rotate(qkv_proj[:, :q_width], cos_table, sin_table))
    key_row_block = low(rotate(qkv_proj[:, q_width:q_width + key_value_width], cos_table, sin_table))
    value_row_block = low(qkv_proj[:, q_width + key_value_width:])
    num_rows = tokens_f.shape[0]
    rows_of_block = min(512, num_rows)
    num_blocks = num_rows // rows_of_block
    row_index = jnp.arange(num_rows, dtype=jnp.int32)
    checked = jax.checkpoint(attend_block)

    def one_block(packed):
        return checked(packed[0], packed[1], packed[2], key_row_block, value_row_block, seg_rows)
    attended = lax.map(one_block, (query_rows.reshape(num_blocks, rows_of_block, q_width), seg_rows.reshape(num_blocks, rows_of_block), row_index.reshape(num_blocks, rows_of_block)))
    attended = low(low_back(attended.reshape(num_rows, q_width)))
    hidden_one = tokens_f + low_back(matmul_hi(attended, w_out))
    normed_two = low(hidden_one * rms_scale(hidden_one) * gain_rows[1])
    gate_up = low_back(matmul_hi(normed_two, w_gu))
    hidden_b = low(jax.nn.silu(gate_up[:, :FF]) * gate_up[:, FF:])
    return hidden_one + low_back(matmul_hi(hidden_b, w_down))

def adamw(weight, first, second, grad, rate, decay):
    first_new = 0.9 * first + 0.1 * grad
    second_new = 0.95 * second + 0.05 * grad * grad
    first_hat = first_new / (1.0 - 0.9 ** STEP)
    second_hat = second_new / (1.0 - 0.95 ** STEP)
    weight_new = weight - rate * (first_hat / (jnp.sqrt(second_hat) + 1e-08) + decay * weight)
    return (first_new, second_new, weight_new)

def reference(tokens, cotangent, segment_ids, positions, projection_weight, projection_first_moment, projection_second_moment, out_weight, out_first, out_second, gate_up_weight, gate_up_first, gate_up_second, down_weight, down_first, down_second, norm_gains, gains_first, gains_second):
    masters = (projection_weight, out_weight, gate_up_weight, down_weight, norm_gains)
    params = tuple((low(weight) for weight in masters))
    num_groups = TOKEN_TOTAL // GROUP_TOKENS
    tokens_g = tokens.astype(jnp.float32).reshape(num_groups, GROUP_TOKENS, MODEL_WIDTH)
    cot_g = cotangent.astype(jnp.float32).reshape(num_groups, GROUP_TOKENS, MODEL_WIDTH)
    seg_g = segment_ids.reshape(num_groups, GROUP_TOKENS)
    pos_g = positions.reshape(num_groups, GROUP_TOKENS)

    def group_step(totals, packed):
        tokens_f, cot_f, seg_rows, pos_rows = packed
        cos_table, sin_table = angles(pos_rows)
        out_f, pull = jax.vjp(lambda prm, inp: layer_forward(prm, inp, seg_rows, cos_table, sin_table), params, tokens_f)
        grad_params, grad_tokens = pull(cot_f)
        totals = tuple((acc + part for acc, part in zip(totals, grad_params)))
        return (totals, (out_f.astype(jnp.bfloat16), grad_tokens.astype(jnp.bfloat16)))
    zeros_init = tuple((jnp.zeros(weight.shape, jnp.float32) for weight in params))
    gradients, (outs_g, grads_g) = lax.scan(group_step, zeros_init, (tokens_g, cot_g, seg_g, pos_g))
    firsts = (projection_first_moment, out_first, gate_up_first, down_first, gains_first)
    seconds = (projection_second_moment, out_second, gate_up_second, down_second, gains_second)
    updated = [adamw(masters[i], firsts[i], seconds[i], gradients[i], RATES[i], DECAYS[i]) for i in range(5)]
    return (outs_g.reshape(TOKEN_TOTAL, MODEL_WIDTH), grads_g.reshape(TOKEN_TOTAL, MODEL_WIDTH), updated[0][0], updated[0][1], updated[0][2], updated[1][0], updated[1][1], updated[1][2], updated[2][0], updated[2][1], updated[2][2], updated[3][0], updated[3][1], updated[3][2], updated[4][0], updated[4][1], updated[4][2])
```

```python
import functools

import jax
import jax.numpy as jnp
from jax import lax
from jax.experimental import pallas as pl
from jax.experimental.pallas import tpu as pltpu
from jax.sharding import PartitionSpec as P

MODEL_WIDTH = 2048
QUERY_HEADS = 32
KEY_VALUE_HEADS = 8
HEAD_SIZE = 64
FF = 8192
STEP = 5


RATES = (0.05, 0.4, 0.05, 0.03, 1.0)
DECAYS = (0.1, 0.1, 0.1, 0.1, 0.0)


def to_bf(value):
    return value.astype(jnp.bfloat16)


def to_f32(value):
    return value.astype(jnp.float32)


def rms_scale(value):
    return lax.rsqrt(jnp.mean(value * value, axis=-1, keepdims=True) + 1e-05)


def tables(position_rows):
    freq = 500000.0 ** (-jnp.arange(HEAD_SIZE // 2, dtype=jnp.float32) * 2.0 / HEAD_SIZE)
    phase = position_rows.astype(jnp.float32)[:, None] * freq[None, :]
    phase = jnp.concatenate([phase, phase], axis=-1)
    return (jnp.cos(phase), jnp.sin(phase))


def rotate(flat, cos_table, sin_table, sign_value):
    num_rows = flat.shape[0]
    half_dim = HEAD_SIZE // 2
    heads = flat.reshape(num_rows, -1, HEAD_SIZE)
    turned = jnp.concatenate([-heads[..., half_dim:], heads[..., :half_dim]], axis=-1)
    return (heads * cos_table[:, None, :] + sign_value * turned * sin_table[:, None, :]).reshape(
        num_rows, -1
    )


def dot(left, right):
    return jnp.dot(left, right, preferred_element_type=jnp.float32)


def contract_last(left, right):
    return lax.dot_general(
        left, right, (((1,), (1,)), ((), ())), preferred_element_type=jnp.float32
    )


def outer_rows(left, right):
    return lax.dot_general(
        left, right, (((0,), (0,)), ((), ())), preferred_element_type=jnp.float32
    )


def norm_back(value, scale_rows, gain_row, grad_normed):
    weighted = grad_normed * gain_row
    inner = jnp.mean(value * weighted, axis=-1, keepdims=True)
    return scale_rows * weighted - value * scale_rows**3 * inner


def adamw(weight, first, second, grad, rate, decay):
    first_new = 0.9 * first + 0.1 * grad
    second_new = 0.95 * second + 0.05 * grad * grad
    first_hat = first_new / (1.0 - 0.9**STEP)
    second_hat = second_new / (1.0 - 0.95**STEP)
    weight_new = weight - rate * (first_hat / (jnp.sqrt(second_hat) + 1e-08) + decay * weight)
    return (first_new, second_new, weight_new)


MESH = pl.DeviceIdType.MESH
VMEM_BYTES = 56 * 1024 * 1024


def after(value, *others):
    return lax.optimization_barrier((value, *others))[0]


def flipped(me, k):
    peer = me
    for bit in (1, 2, 4):
        mine = lax.rem(lax.div(me, jnp.int32(bit)), jnp.int32(2))
        if isinstance(k, int):
            on = (k // bit) % 2
            if not on:
                continue
        else:
            on = lax.rem(lax.div(k, jnp.int32(bit)), jnp.int32(2))
        peer = peer + on * bit * (1 - 2 * mine)
    return peer


def call_peers(peers):
    barrier = pltpu.get_barrier_semaphore()
    for peer in peers:
        pl.semaphore_signal(barrier, inc=1, device_id={"rep": peer}, device_id_type=MESH)


def await_peers(peers):
    pl.semaphore_wait(pltpu.get_barrier_semaphore(), len(peers))


def remote(src, dst, sems, index, peer):
    return pltpu.make_async_remote_copy(
        src_ref=src,
        dst_ref=dst,
        send_sem=sems[0].at[index],
        recv_sem=sems[1].at[index],
        device_id={"rep": peer},
        device_id_type=MESH,
    )


def swap_halves(value):
    return pltpu.roll(value, HEAD_SIZE, axis=1)


def head_at(rows, head, low_half):
    pair = to_f32(rows[:, (head // 2) * 128 : (head // 2) * 128 + 128])
    if (head % 2 == 0) != low_half:
        pair = swap_halves(pair)
    lane = lax.broadcasted_iota(jnp.int32, pair.shape, 1)
    keep = lane < HEAD_SIZE if low_half else lane >= HEAD_SIZE
    return to_bf(jnp.where(keep, pair, 0.0))


def joined(even, odd, low_half):
    lane = lax.broadcasted_iota(jnp.int32, even.shape, 1)
    if low_half:
        return jnp.where(lane < HEAD_SIZE, even, swap_halves(odd))
    return jnp.where(lane < HEAD_SIZE, swap_halves(even), odd)


def lower_keys(kv_ref):
    lines, rows, wide = kv_ref.shape
    kv = to_f32(kv_ref[...].reshape(lines * rows, wide))
    came = lax.broadcasted_iota(jnp.int32, kv.shape, 0) < (lax.axis_index("shard") + 1) * rows
    return to_bf(jnp.where(came, kv, 0.0))


def turned_pair(both):
    lane = lax.broadcasted_iota(jnp.int32, both.shape, 1)
    low = lax.rem(lane, jnp.int32(HEAD_SIZE)) < HEAD_SIZE // 2
    back = pltpu.roll(both, 128 - HEAD_SIZE // 2, axis=1)
    return jnp.where(low, -back, pltpu.roll(both, HEAD_SIZE // 2, axis=1))


def angle_pair(table):
    count = HEAD_SIZE // 2
    return [
        jnp.concatenate([table[:, at : at + count]] * 4, axis=1) for at in (0, count)
    ]


def project_kernel(x_ref, w_ref, gain_ref, table_ref, normed_ref, q_ref, kv_ref):
    x = to_f32(x_ref[0])
    normed = to_bf(x * rms_scale(x) * gain_ref[...])
    normed_ref[0] = normed
    qkv = dot(normed, w_ref[...])
    cos_pair, sin_pair = angle_pair(table_ref[0])

    def turn(pair):
        return pair * cos_pair + turned_pair(pair) * sin_pair

    for pair in range(2):
        at = slice(pair * 128, pair * 128 + 128)
        q_ref[:, at] = to_bf(to_f32(to_bf(turn(qkv[:, at]))) * HEAD_SIZE**-0.5)
    key_value = qkv[:, 256:384]
    lane = lax.broadcasted_iota(jnp.int32, key_value.shape, 1)
    kv_ref[...] = to_bf(jnp.where(lane < HEAD_SIZE, turn(key_value), key_value))


def project(tokens_all, weights, gain, table):
    _, rows, depth = tokens_all.shape
    bf = jnp.bfloat16
    return pl.pallas_call(
        project_kernel,
        grid=(8,),
        in_specs=[
            pl.BlockSpec((1, rows, depth), lambda i: (i, 0, 0)),
            pl.BlockSpec((depth, 384), lambda i: (0, 0)),
            pl.BlockSpec((1, depth), lambda i: (0, 0)),
            pl.BlockSpec((1, rows, 128), lambda i: (i, 0, 0)),
        ],
        out_specs=[
            pl.BlockSpec((1, rows, depth), lambda i: (i, 0, 0)),
            pl.BlockSpec((rows, 256), lambda i: (i, 0)),
            pl.BlockSpec((rows, 128), lambda i: (i, 0)),
        ],
        out_shape=[
            jax.ShapeDtypeStruct((8, rows, depth), bf),
            jax.ShapeDtypeStruct((8 * rows, 256), bf),
            jax.ShapeDtypeStruct((8 * rows, 128), bf),
        ],
        compiler_params=pltpu.CompilerParams(vmem_limit_bytes=VMEM_BYTES),
        name="project",
    )(tokens_all, weights, gain, table)


def attend_kernel(q_ref, kv_ref, seg_q_ref, seg_k_ref, own_ref, log_ref, sent_ref, out_buf, send, recv, local):
    step = pl.program_id(0)
    slot = 7 - step
    me = lax.axis_index("rep")
    peers = [flipped(me, k) for k in range(1, 8)]
    rows = q_ref.shape[0]
    keys = kv_ref.shape[0] * kv_ref.shape[1]

    @pl.when(step == 0)
    def _():
        call_peers(peers)

    kv = lower_keys(kv_ref)
    row_at = lax.axis_index("shard") * rows + lax.broadcasted_iota(jnp.int32, (rows, keys), 0)
    key_at = lax.broadcasted_iota(jnp.int32, (rows, keys), 1)
    allowed = (seg_q_ref[0] == seg_k_ref[0]) & (key_at <= row_at)
    bias = jnp.where(allowed, 0.0, -1e30)
    q = q_ref[...]
    outs = []
    for head in range(4):
        scores = contract_last(head_at(q, head, True), kv) + bias
        peak = jnp.max(scores, axis=1, keepdims=True)
        probs = jnp.exp(scores - peak)
        total = jnp.sum(probs, axis=1, keepdims=True)
        log_ref[0, :, head : head + 1] = peak + jnp.log(total)
        outs.append(dot(to_bf(probs), kv) * (1.0 / total))
    for pair in range(2):
        out_buf[slot, :, pair * 128 : pair * 128 + 128] = to_bf(
            joined(outs[2 * pair], outs[2 * pair + 1], False)
        )
    own_ref[...] = out_buf[slot]

    @pl.when(step == 0)
    def _():
        await_peers(peers)

    def copy(k):
        place = sent_ref.at[:, pl.ds(pl.multiple_of(k * 256, 256), 256)]
        return remote(out_buf.at[k], place, (send, recv), k, flipped(me, k))

    @pl.when(slot > 0)
    def _():
        copy(slot).start()

    @pl.when(slot == 0)
    def _():
        mine = pltpu.make_async_copy(out_buf.at[0], sent_ref.at[:, pl.ds(0, 256)], local)
        mine.start()
        for k in range(1, 8):
            copy(k).wait()
        mine.wait()


def attend(q, kv_line, seg_q, seg_k):
    lines, plane, _ = kv_line.shape
    rows = plane // 8
    return pl.pallas_call(
        attend_kernel,
        grid=(8,),
        in_specs=[
            pl.BlockSpec((rows, 256), lambda i: (7 - i, 0)),
            pl.BlockSpec((lines, rows, 128), lambda i: (0, 7 - i, 0)),
            pl.BlockSpec((1, rows, 1), lambda i: (7 - i, 0, 0)),
            pl.BlockSpec((1, 1, lines * rows), lambda i: (7 - i, 0, 0)),
        ],
        out_specs=[
            pl.BlockSpec((rows, 256), lambda i: (7 - i, 0)),
            pl.BlockSpec((1, rows, 4), lambda i: (7 - i, 0, 0)),
            pl.BlockSpec(memory_space=pl.ANY),
        ],
        out_shape=[
            jax.ShapeDtypeStruct((plane, 256), jnp.bfloat16),
            jax.ShapeDtypeStruct((8, rows, 4), jnp.float32),
            jax.ShapeDtypeStruct((rows, 2048), jnp.bfloat16),
        ],
        scratch_shapes=[
            pltpu.VMEM((8, rows, 256), jnp.bfloat16),
            pltpu.SemaphoreType.DMA((8,)),
            pltpu.SemaphoreType.DMA((8,)),
            pltpu.SemaphoreType.DMA,
        ],
        compiler_params=pltpu.CompilerParams(
            collective_id=1, has_side_effects=True, vmem_limit_bytes=VMEM_BYTES
        ),
        name="attend",
    )(q, kv_line, seg_q, seg_k)


def attend_back_kernel(
    d_ref, q_ref, kv_ref, seg_q_ref, seg_k_ref, log_ref, table_ref, block_ref,
    dq_ref, dkv_ref, blocks_ref,
    d_buf, send, recv, local, block_send, block_recv, block_local,
):
    slot = pl.program_id(0)
    me = lax.axis_index("rep")
    peers = [flipped(me, k) for k in range(1, 8)]
    rows = q_ref.shape[0]
    lines = kv_ref.shape[0]
    keys = lines * kv_ref.shape[1]

    def copy(k):
        piece = d_ref.at[:, pl.ds(pl.multiple_of(k * 256, 256), 256)]
        return remote(piece, d_buf.at[k], (send, recv), k, flipped(me, k))

    spread = Spread(
        me, block_ref, lambda k: blocks_ref.at[k], (block_send, block_recv), block_local
    )

    @pl.when(slot == 0)
    def _():
        call_peers(peers)
        mine = pltpu.make_async_copy(d_ref.at[:, pl.ds(0, 256)], d_buf.at[0], local)
        mine.start()
        await_peers(peers)
        for k in range(1, 8):
            copy(k).start()
        spread.begin()
        mine.wait()

    @pl.when(slot > 0)
    def _():
        copy(slot).wait_recv()

    @pl.when(slot == 5)
    def _():
        spread.middle()

    kv = lower_keys(kv_ref)
    key_at = lax.broadcasted_iota(jnp.int32, (keys, rows), 0)
    row_at = lax.axis_index("shard") * rows + lax.broadcasted_iota(jnp.int32, (keys, rows), 1)
    allowed = (seg_k_ref[0] == seg_q_ref[0]) & (key_at <= row_at)
    bias = jnp.where(allowed, 0.0, -1e30)
    q = q_ref[...]
    d_out = d_buf[slot]
    grads = []
    dkv = jnp.zeros((keys, 128), jnp.float32)
    for head in range(4):
        q_one = head_at(q, head, True)
        d_one = head_at(d_out, head, False)
        probs = jnp.exp(contract_last(kv, q_one) + bias - log_ref[0, head : head + 1, :])
        grad_probs = contract_last(kv, d_one)
        inner = jnp.sum(grad_probs * probs, axis=0, keepdims=True)
        grad_scores = to_bf(probs * (grad_probs - inner))
        grads.append(outer_rows(grad_scores, kv))
        dkv = dkv + dot(grad_scores, q_one) + dot(to_bf(probs), d_one)
    cos_pair, sin_pair = angle_pair(table_ref[0])
    for pair in range(2):
        both = joined(grads[2 * pair], grads[2 * pair + 1], True) * (HEAD_SIZE**-0.5)
        dq_ref[:, pair * 128 : pair * 128 + 128] = to_bf(
            both * cos_pair - turned_pair(both) * sin_pair
        )
    dkv_ref[...] = to_bf(dkv).reshape(lines, rows, 128)

    @pl.when(slot == 7)
    def _():
        for k in range(1, 8):
            copy(k).wait_send()
        spread.last()
        spread.end()


def attend_back(d_own, block, q, kv_line, seg_q, seg_k, logs, table):
    lines, plane, _ = kv_line.shape
    rows = plane // 8
    bf = jnp.bfloat16
    return pl.pallas_call(
        attend_back_kernel,
        grid=(8,),
        in_specs=[
            pl.BlockSpec(memory_space=pl.ANY),
            pl.BlockSpec((rows, 256), lambda i: (i, 0)),
            pl.BlockSpec((lines, rows, 128), lambda i: (0, i, 0)),
            pl.BlockSpec((1, 1, rows), lambda i: (i, 0, 0)),
            pl.BlockSpec((1, lines * rows, 1), lambda i: (i, 0, 0)),
            pl.BlockSpec((1, 4, rows), lambda i: (i, 0, 0)),
            pl.BlockSpec((1, rows, 128), lambda i: (i, 0, 0)),
            pl.BlockSpec(memory_space=pl.ANY),
        ],
        out_specs=[
            pl.BlockSpec((rows, 256), lambda i: (i, 0)),
            pl.BlockSpec((lines, rows, 128), lambda i: (0, i, 0)),
            pl.BlockSpec(memory_space=pl.ANY),
        ],
        out_shape=[
            jax.ShapeDtypeStruct((plane, 256), bf),
            jax.ShapeDtypeStruct((lines, plane, 128), bf),
            jax.ShapeDtypeStruct((8, *block.shape), block.dtype),
        ],
        scratch_shapes=[
            pltpu.VMEM((8, rows, 256), bf),
            pltpu.SemaphoreType.DMA((8,)),
            pltpu.SemaphoreType.DMA((8,)),
            pltpu.SemaphoreType.DMA,
            pltpu.SemaphoreType.DMA((7,)),
            pltpu.SemaphoreType.DMA((7,)),
            pltpu.SemaphoreType.DMA,
        ],
        compiler_params=pltpu.CompilerParams(
            collective_id=2, has_side_effects=True, vmem_limit_bytes=VMEM_BYTES
        ),
        name="attend_back",
    )(d_own, q, kv_line, seg_q, seg_k, logs, table, block)


def corner_route(me):
    core = lax.rem(me, jnp.int32(2))
    first, second = 2 + 2 * core, 4 - 2 * core
    return first, second, flipped(me, 1), flipped(me, first), flipped(me, second)


class Spread:
    def __init__(self, me, source, place, sems, local):
        first, second, sibling, one, two = corner_route(me)
        self.own = lambda: pltpu.make_async_copy(source, place(0), local)
        self.to_sibling = lambda: remote(source, place(1), sems, 0, sibling)
        self.to_one = lambda: remote(source, place(first), sems, 1, one)
        self.to_two = lambda: remote(source, place(second), sems, 2, two)
        self.corner = lambda: remote(place(second), place(6), sems, 3, one)
        self.pass_first = lambda: remote(place(first), place(first + 1), sems, 4, sibling)
        self.pass_second = lambda: remote(place(second), place(second + 1), sems, 5, sibling)
        self.pass_corner = lambda: remote(place(6), place(7), sems, 6, sibling)

    def begin(self):
        self.own().start()
        self.to_one().start()
        self.to_two().start()
        self.to_sibling().start()

    def middle(self):
        self.to_two().wait_recv()
        self.corner().start()
        self.pass_second().start()
        self.to_one().wait_recv()
        self.pass_first().start()

    def last(self):
        self.corner().wait_recv()
        self.pass_corner().start()

    def end(self):
        for move in (self.to_sibling, self.pass_first, self.pass_second, self.pass_corner):
            move().wait_recv()
        for move in (
            self.to_one,
            self.to_two,
            self.to_sibling,
            self.corner,
            self.pass_first,
            self.pass_second,
            self.pass_corner,
        ):
            move().wait_send()
        self.own().wait()


def gather_kernel(columns, *refs):
    count = len(columns)
    sources, outs = refs[:count], refs[count : 2 * count]
    send, recv, local = refs[2 * count :]
    me = lax.axis_index("rep")
    peers = [flipped(me, k) for k in (1, 2, 4)]
    call_peers(peers)

    def spread(i):
        source = sources[i]
        if columns[i] is None:
            return Spread(me, source, lambda k: outs[i].at[k], (send.at[i], recv.at[i]), local.at[i])
        start, width = columns[i]

        def place(k):
            return outs[i].at[:, pl.ds(pl.multiple_of(k * width, width), width)]

        source = source.at[:, pl.ds(start, width)]
        return Spread(me, source, place, (send.at[i], recv.at[i]), local.at[i])

    spreads = [spread(i) for i in range(count)]
    await_peers(peers)
    for one in spreads:
        one.begin()
    for one in spreads:
        one.middle()
    for one in spreads:
        one.last()
    for one in spreads:
        one.end()


def plane_gather(blocks, columns, number):
    count = len(blocks)
    shapes = [
        (8, *b.shape) if c is None else (b.shape[0], 8 * c[1]) for b, c in zip(blocks, columns)
    ]
    return pl.pallas_call(
        functools.partial(gather_kernel, columns),
        in_specs=[pl.BlockSpec(memory_space=pl.ANY)] * count,
        out_specs=[pl.BlockSpec(memory_space=pl.ANY)] * count,
        out_shape=[jax.ShapeDtypeStruct(s, b.dtype) for s, b in zip(shapes, blocks)],
        scratch_shapes=[
            pltpu.SemaphoreType.DMA((count, 7)),
            pltpu.SemaphoreType.DMA((count, 7)),
            pltpu.SemaphoreType.DMA((count,)),
        ],
        compiler_params=pltpu.CompilerParams(collective_id=number, has_side_effects=True),
        name=f"plane_gather_{number}",
    )(*blocks)


def call_line(line, count):
    barrier = pltpu.get_barrier_semaphore()
    for step in (1, count - 1):
        peer = lax.rem(line + step, jnp.int32(count))
        pl.semaphore_signal(barrier, inc=1, device_id={"shard": peer}, device_id_type=MESH)


def await_plane_and_line():
    pl.semaphore_wait(pltpu.get_barrier_semaphore(), 5)


def line_copy(src, dst, sems, index, peer):
    return pltpu.make_async_remote_copy(
        src_ref=src,
        dst_ref=dst,
        send_sem=sems[0].at[index],
        recv_sem=sems[1].at[index],
        device_id={"shard": peer},
        device_id_type=MESH,
    )


KEY_PIECES = 4


def gather_keys_kernel(
    columns, w_ref, dy_ref, kv_ref, slots_ref, dy_all_ref, line_ref,
    send, recv, local, line_send, line_recv, line_local,
):
    me = lax.axis_index("rep")
    line = lax.axis_index("shard")
    count = line_ref.shape[0]
    start, width = columns
    piece = kv_ref.shape[0] // KEY_PIECES
    call_peers([flipped(me, k) for k in (1, 2, 4)])
    call_line(line, count)

    def place(k):
        return slots_ref.at[:, pl.ds(pl.multiple_of(k * width, width), width)]

    weights = Spread(
        me, w_ref.at[:, pl.ds(start, width)], place, (send.at[0], recv.at[0]), local.at[0]
    )
    blocks = Spread(
        me, dy_ref, lambda k: dy_all_ref.at[k], (send.at[1], recv.at[1]), local.at[1]
    )
    mine = pltpu.make_async_copy(kv_ref, line_ref.at[line], line_local)
    mine.start()

    def forward(step, part):
        rows = pl.ds(part * piece, piece)
        dst = line_ref.at[line - step, rows]
        src = kv_ref.at[rows] if step == 0 else dst
        sems = (line_send.at[step], line_recv.at[step])
        return line_copy(src, dst, sems, part, line + 1)

    def arrival(step, part):
        dst = line_ref.at[line - 1 - step, pl.ds(part * piece, piece)]
        return line_copy(dst, dst, (line_send.at[step], line_recv.at[step]), part, line - 1)

    def await_arrival(step, part):
        @pl.when(line >= step + 1)
        def _():
            arrival(step, part).wait_recv()

    def start_forward(step, part):
        @pl.when((line >= step) & (line < count - 1))
        def _():
            forward(step, part).start()

    await_plane_and_line()
    for part in range(KEY_PIECES):
        start_forward(0, part)
    weights.begin()
    blocks.begin()
    for step in range(1, count - 1):
        for part in range(KEY_PIECES):
            await_arrival(step - 1, part)
            start_forward(step, part)
        if step == 1:
            weights.middle()
        if step == 2:
            blocks.middle()
    weights.last()
    blocks.last()
    weights.end()
    blocks.end()
    for part in range(KEY_PIECES):
        await_arrival(count - 2, part)
    for step in range(count - 1):

        @pl.when((line >= step) & (line < count - 1))
        def _():
            for part in range(KEY_PIECES):
                forward(step, part).wait_send()

    mine.wait()


def gather_keys(weights, columns, block, kv_own, count, number):
    return pl.pallas_call(
        functools.partial(gather_keys_kernel, columns),
        in_specs=[pl.BlockSpec(memory_space=pl.ANY)] * 3,
        out_specs=[pl.BlockSpec(memory_space=pl.ANY)] * 3,
        out_shape=[
            jax.ShapeDtypeStruct((weights.shape[0], 8 * columns[1]), weights.dtype),
            jax.ShapeDtypeStruct((8, *block.shape), block.dtype),
            jax.ShapeDtypeStruct((count, *kv_own.shape), kv_own.dtype),
        ],
        scratch_shapes=[
            pltpu.SemaphoreType.DMA((2, 7)),
            pltpu.SemaphoreType.DMA((2, 7)),
            pltpu.SemaphoreType.DMA((2,)),
            pltpu.SemaphoreType.DMA((count - 1, KEY_PIECES)),
            pltpu.SemaphoreType.DMA((count - 1, KEY_PIECES)),
            pltpu.SemaphoreType.DMA,
        ],
        compiler_params=pltpu.CompilerParams(collective_id=number, has_side_effects=True),
        name="gather_keys",
    )(weights, block, kv_own)


def column_slice(ref, start, width):
    return ref[:, pl.ds(pl.multiple_of(start, width), width)]


def send_all(me, peers, bufs, places, sems, local):
    count = len(bufs)
    own = [
        pltpu.make_async_copy(bufs[i].at[0], places[i](0), local.at[i]) for i in range(count)
    ]
    moves = [
        [
            remote(bufs[i].at[k], places[i](k), (sems[0].at[i], sems[1].at[i]), k, peers[k - 1])
            for k in (7, 6, 5, 4, 3, 2, 1)
        ]
        for i in range(count)
    ]
    for i in range(count):
        own[i].start()
        for move in moves[i]:
            move.start()
    for i in range(count):
        for move in moves[i]:
            move.wait()
        own[i].wait()


def swap_first_kernel(proj_ref, out_w_ref, out_ref, buf, send, recv, local):
    me = lax.axis_index("rep")
    peers = [flipped(me, k) for k in range(1, 8)]
    call_peers(peers)
    q_all = QUERY_HEADS * HEAD_SIZE
    kv_all = KEY_VALUE_HEADS * HEAD_SIZE
    for k in range(8):
        to = peers[k - 1] if k else me
        odd = lax.rem(to, jnp.int32(2)) == 1
        pair = lax.div(to, jnp.int32(2)) * 128
        key = column_slice(proj_ref, q_all + pair, 128)
        value = column_slice(proj_ref, q_all + kv_all + pair, 128)
        lane = lax.broadcasted_iota(jnp.int32, key.shape, 1)
        key = jnp.where(odd, swap_halves(key), key)
        value = jnp.where(odd, value, swap_halves(value))
        buf[k, :, 0:256] = to_bf(column_slice(proj_ref, to * 256, 256))
        buf[k, :, 256:384] = to_bf(jnp.where(lane < HEAD_SIZE, key, value))
        buf[k, :, 384:640] = to_bf(column_slice(out_w_ref, to * 256, 256))
    await_peers(peers)
    send_all(me, peers, (buf,), (lambda k: out_ref.at[me],), (send, recv), local)


def swap_first(proj_w, out_w_t):
    owned = proj_w.shape[0]
    return pl.pallas_call(
        swap_first_kernel,
        in_specs=[pl.BlockSpec(memory_space=pltpu.VMEM)] * 2,
        out_specs=pl.BlockSpec(memory_space=pl.ANY),
        out_shape=jax.ShapeDtypeStruct((8, owned, 640), jnp.bfloat16),
        scratch_shapes=[
            pltpu.VMEM((8, owned, 640), jnp.bfloat16),
            pltpu.SemaphoreType.DMA((1, 8)),
            pltpu.SemaphoreType.DMA((1, 8)),
            pltpu.SemaphoreType.DMA((1,)),
        ],
        compiler_params=pltpu.CompilerParams(
            collective_id=7, has_side_effects=True, vmem_limit_bytes=VMEM_BYTES
        ),
        name="swap_first",
    )(proj_w, out_w_t)


def swap_ffn_kernel(gu_ref, down_ref, out_a, out_b, buf_a, buf_b, send, recv, local):
    me = lax.axis_index("rep")
    peers = [flipped(me, k) for k in range(1, 8)]
    call_peers(peers)
    for half, buf in enumerate((buf_a, buf_b)):
        for k in range(8):
            to = peers[k - 1] if k else me
            at = half * (FF // 2) + to * 512
            buf[k, :, 0:512] = to_bf(column_slice(gu_ref, at, 512))
            buf[k, :, 512:1024] = to_bf(column_slice(gu_ref, FF + at, 512))
            buf[k, :, 1024:1536] = to_bf(column_slice(down_ref, at, 512))
    await_peers(peers)
    send_all(
        me,
        peers,
        (buf_a, buf_b),
        (lambda k: out_a.at[me], lambda k: out_b.at[me]),
        (send, recv),
        local,
    )


def swap_ffn(gu_w, down_w_t):
    owned = gu_w.shape[0]
    wide = (8, owned, 1536)
    return pl.pallas_call(
        swap_ffn_kernel,
        in_specs=[pl.BlockSpec(memory_space=pltpu.VMEM)] * 2,
        out_specs=[pl.BlockSpec(memory_space=pl.ANY)] * 2,
        out_shape=[jax.ShapeDtypeStruct(wide, jnp.bfloat16)] * 2,
        scratch_shapes=[
            pltpu.VMEM(wide, jnp.bfloat16),
            pltpu.VMEM(wide, jnp.bfloat16),
            pltpu.SemaphoreType.DMA((2, 8)),
            pltpu.SemaphoreType.DMA((2, 8)),
            pltpu.SemaphoreType.DMA((2,)),
        ],
        compiler_params=pltpu.CompilerParams(
            collective_id=8, has_side_effects=True, vmem_limit_bytes=VMEM_BYTES
        ),
        name="swap_ffn",
    )(gu_w, down_w_t)


def swap_back_kernel(layout, *refs):
    outs = 1 + max(entry[3] for entry in layout)
    sources, results = refs, refs[-3 - outs : -3]
    send, recv, local = refs[-3:]
    me = lax.axis_index("rep")
    peers = [flipped(me, k) for k in range(1, 8)]
    call_peers(peers)
    own, moves = [], []
    for n, (i, start, width, o, at) in enumerate(layout):

        def piece(to):
            return sources[i].at[to, :, pl.ds(start, width)]

        place = results[o].at[:, pl.ds(pl.multiple_of(at + me * width, 128), width)]
        own.append(pltpu.make_async_copy(piece(me), place, local.at[n]))
        moves.append(
            [
                remote(piece(peers[k - 1]), place, (send.at[n], recv.at[n]), k, peers[k - 1])
                for k in (7, 6, 5, 4, 3, 2, 1)
            ]
        )
    for move in own:
        move.start()
    await_peers(peers)
    for group in moves:
        for move in group:
            move.start()
    for group, mine in zip(moves, own):
        for move in group:
            move.wait()
        mine.wait()


def swap_back(sources, layout, widths, number, earlier=()):
    aliases = {len(sources) + i: i for i in range(len(earlier))}
    sources = [source.reshape(8, -1, source.shape[1]) for source in sources]
    owned = sources[0].shape[1]
    return pl.pallas_call(
        functools.partial(swap_back_kernel, layout),
        in_specs=[pl.BlockSpec(memory_space=pl.ANY)] * (len(sources) + len(earlier)),
        out_specs=[pl.BlockSpec(memory_space=pl.ANY)] * len(widths),
        out_shape=[jax.ShapeDtypeStruct((owned, width), jnp.bfloat16) for width in widths],
        input_output_aliases=aliases,
        scratch_shapes=[
            pltpu.SemaphoreType.DMA((len(layout), 8)),
            pltpu.SemaphoreType.DMA((len(layout), 8)),
            pltpu.SemaphoreType.DMA((len(layout),)),
        ],
        compiler_params=pltpu.CompilerParams(collective_id=number, has_side_effects=True),
        name=f"swap_back_{number}",
    )(*sources, *earlier)


def ffn_first_kernel(
    x_ref, dy_ref, w_ref, xall_ref, hid_ref, dgu_ref,
    x_buf, dy_buf, w_buf, hid_buf, dgu_buf, send, recv, w_sem, dy_sem, x_sem, out_sem,
):
    me = lax.axis_index("rep")
    first, second, sibling, one, two = corner_route(me)
    peers = [flipped(me, k) for k in (1, 2, 4)]
    width = hid_ref.shape[2]
    sems = (send, recv)
    loads = [
        pltpu.make_async_copy(w_ref.at[:, pl.ds(i * width, width)], w_buf.at[i], w_sem.at[i])
        for i in range(3)
    ]

    def dy_load(k):
        return pltpu.make_async_copy(dy_ref.at[k], dy_buf.at[k], dy_sem.at[k])

    call_peers(peers)
    mine = pltpu.make_async_copy(x_ref, x_buf.at[0], x_sem.at[0])
    mine.start()
    dy_load(0).start()
    for copy in loads:
        copy.start()
    for k in range(1, 8):
        dy_load(k).start()
    to_sibling = remote(x_buf.at[0], x_buf.at[1], sems, 0, sibling)
    to_one = remote(x_buf.at[0], x_buf.at[first], sems, 1, one)
    to_two = remote(x_buf.at[0], x_buf.at[second], sems, 2, two)
    corner = remote(x_buf.at[second], x_buf.at[6], sems, 3, one)
    pass_first = remote(x_buf.at[first], x_buf.at[first + 1], sems, 4, sibling)
    pass_second = remote(x_buf.at[second], x_buf.at[second + 1], sems, 5, sibling)
    pass_corner = remote(x_buf.at[6], x_buf.at[7], sems, 6, sibling)
    mine.wait()
    await_peers(peers)
    to_one.start()
    to_two.start()
    to_sibling.start()
    for copy in loads:
        copy.wait()

    def results(k):
        return (
            pltpu.make_async_copy(hid_buf.at[k], hid_ref.at[k], out_sem.at[0, k]),
            pltpu.make_async_copy(dgu_buf.at[k], dgu_ref.at[k], out_sem.at[1, k]),
        )

    def work(k):
        dy_load(k).wait()

        @pl.loop(0, width // 256)
        def _(j):
            at = pl.multiple_of(j * 256, 256)
            cols = pl.ds(at, 256)
            x = x_buf[k]
            gate = dot(x, w_buf[0, :, cols])
            up = dot(x, w_buf[1, :, cols])
            grad_hidden = dot(dy_buf[k], w_buf[2, :, cols])
            sig = 1.0 / (1.0 + jnp.exp(-gate))
            silu = gate * sig
            hid_buf[k, :, cols] = to_bf(silu * up)
            dgu_buf[k, :, cols] = to_bf(grad_hidden * up * sig * (1.0 + gate * (1.0 - sig)))
            dgu_buf[k, :, pl.ds(width + at, 256)] = to_bf(grad_hidden * silu)

        for copy in results(k):
            copy.start()

    work(0)
    to_sibling.wait_recv()
    work(1)
    to_two.wait_recv()
    corner.start()
    pass_second.start()
    to_one.wait_recv()
    pass_first.start()
    work(first)
    work(second)
    pass_first.wait_recv()
    work(second + 1)
    corner.wait_recv()
    pass_corner.start()
    pass_second.wait_recv()
    work(first + 1)
    work(6)
    pass_corner.wait_recv()
    keep = pltpu.make_async_copy(x_buf, xall_ref, x_sem.at[1])
    keep.start()
    work(7)
    for copy in (to_sibling, to_one, to_two, corner, pass_first, pass_second, pass_corner):
        copy.wait_send()
    keep.wait()

    for k in range(8):
        for copy in results(k):
            copy.wait()


def ffn_first(x, dy_all, weights):
    _, rows, depth = dy_all.shape
    width = weights.shape[1] // 3
    shapes = [(8, rows, depth), (8, rows, width), (8, rows, 2 * width)]
    return pl.pallas_call(
        ffn_first_kernel,
        in_specs=[pl.BlockSpec(memory_space=pl.ANY)] * 3,
        out_specs=[pl.BlockSpec(memory_space=pl.ANY)] * 3,
        out_shape=[jax.ShapeDtypeStruct(shape, jnp.bfloat16) for shape in shapes],
        scratch_shapes=[
            pltpu.VMEM((8, rows, depth), jnp.bfloat16),
            pltpu.VMEM((8, rows, depth), jnp.bfloat16),
            pltpu.VMEM((3, depth, width), jnp.bfloat16),
            pltpu.VMEM((8, rows, width), jnp.bfloat16),
            pltpu.VMEM((8, rows, 2 * width), jnp.bfloat16),
            pltpu.SemaphoreType.DMA((7,)),
            pltpu.SemaphoreType.DMA((7,)),
            pltpu.SemaphoreType.DMA((3,)),
            pltpu.SemaphoreType.DMA((8,)),
            pltpu.SemaphoreType.DMA((2,)),
            pltpu.SemaphoreType.DMA((2, 8)),
        ],
        compiler_params=pltpu.CompilerParams(
            collective_id=3, has_side_effects=True, vmem_limit_bytes=VMEM_BYTES
        ),
        name="ffn_first",
    )(x, dy_all, weights)


def ffn_gradient_kernel(x_ref, dy_ref, dgu_ref, hid_ref, out_ref):
    rows = x_ref.shape[0] * x_ref.shape[1]
    x = x_ref[...].reshape(rows, -1)
    dy = dy_ref[...].reshape(rows, -1)
    both = dgu_ref.shape[2]
    for at in range(0, both, 512):
        part = dgu_ref[:, :, at : at + 512].reshape(rows, -1)
        out_ref[:, at : at + 512] = to_bf(outer_rows(x, part))
    out_ref[:, both:] = to_bf(outer_rows(dy, hid_ref[...].reshape(rows, -1)))


def ffn_gradient(x_all, dy_all, dgu, hid):
    slots, rows, depth = x_all.shape
    both, width = dgu.shape[2], hid.shape[2]
    return pl.pallas_call(
        ffn_gradient_kernel,
        grid=(depth // 256,),
        in_specs=[
            pl.BlockSpec((slots, rows, 256), lambda i: (0, 0, i)),
            pl.BlockSpec((slots, rows, 256), lambda i: (0, 0, i)),
            pl.BlockSpec((slots, rows, both), lambda i: (0, 0, 0)),
            pl.BlockSpec((slots, rows, width), lambda i: (0, 0, 0)),
        ],
        out_specs=pl.BlockSpec((256, both + width), lambda i: (i, 0)),
        out_shape=jax.ShapeDtypeStruct((depth, both + width), jnp.bfloat16),
        compiler_params=pltpu.CompilerParams(vmem_limit_bytes=VMEM_BYTES),
        name="ffn_gradient",
    )(x_all, dy_all, dgu, hid)


def ffn_second_kernel(
    x_ref, dy_ref, w_ref, hid_a_ref, dgu_a_ref, w_a_ref, hid_ref, dgu_ref, out_ref, layer_ref,
    x_buf, dy_buf, w_buf, wa_buf, hid_a_buf, dgu_a_buf, hid_buf, dgu_buf,
    to_buf, from_buf, layer_to, layer_from,
    send, recv, layer_send, layer_recv, w_sem, in_sem, out_sem,
):
    me = lax.axis_index("rep")
    peers = [flipped(me, k) for k in (1, 2, 4)]
    call_peers(peers)
    width = hid_ref.shape[2]
    loads = [
        pltpu.make_async_copy(w_ref.at[:, pl.ds(i * width, width)], w_buf.at[i], w_sem.at[i])
        for i in range(3)
    ]
    loads.append(pltpu.make_async_copy(w_a_ref, wa_buf, w_sem.at[3]))

    def block_loads(n, k):
        pairs = (
            (x_ref, x_buf), (dy_ref, dy_buf), (hid_a_ref, hid_a_buf), (dgu_a_ref, dgu_a_buf)
        )
        return [
            pltpu.make_async_copy(ref.at[k], buf.at[n % 2], in_sem.at[i, n % 2])
            for i, (ref, buf) in enumerate(pairs)
        ]

    def results(n, k):
        gate_at, up_at = pl.ds(0, width), pl.ds(width, width)
        pairs = (
            (hid_buf.at[n % 2], hid_ref.at[k]),
            (dgu_buf.at[0, n % 2], dgu_ref.at[k, :, gate_at]),
            (dgu_buf.at[1, n % 2], dgu_ref.at[k, :, up_at]),
        )
        return [
            pltpu.make_async_copy(src, dst, out_sem.at[i, n % 2])
            for i, (src, dst) in enumerate(pairs)
        ]

    def work(n):
        def tile(at):
            x = x_buf[n % 2]
            gate = dot(x, w_buf[0, :, at])
            up = dot(x, w_buf[1, :, at])
            grad_hidden = dot(dy_buf[n % 2], w_buf[2, :, at])
            sig = 1.0 / (1.0 + jnp.exp(-gate))
            silu = gate * sig
            hid_buf[n % 2, :, at] = to_bf(silu * up)
            dgu_buf[0, n % 2, :, at] = to_bf(grad_hidden * up * sig * (1.0 + gate * (1.0 - sig)))
            dgu_buf[1, n % 2, :, at] = to_bf(grad_hidden * silu)

        column_tiles(width // 256, tile)

    gate_up_at, down_at = pl.ds(0, 2 * width), pl.ds(2 * width, width)
    turn = [0]

    def product(k, write):
        n = turn[0]

        def tile(at):
            value = contract_last(dgu_a_buf[n % 2], wa_buf[at, gate_up_at])
            value = value + contract_last(dgu_buf[0, n % 2], w_buf[0, at, :])
            write(at, value + contract_last(dgu_buf[1, n % 2], w_buf[1, at, :]))

        column_tiles(out_ref.shape[1] // 256, tile)

    def layer_product(k, write):
        n = turn[0]

        def tile(at):
            value = contract_last(hid_a_buf[n % 2], wa_buf[at, down_at])
            write(at, value + contract_last(hid_buf[n % 2], w_buf[2, at, :]))

        column_tiles(out_ref.shape[1] // 256, tile)

    total = PlaneSum(me, product, out_ref, to_buf, from_buf, (send, recv))
    layer = PlaneSum(me, layer_product, layer_ref, layer_to, layer_from, (layer_send, layer_recv))
    for copy in (*block_loads(0, total.order[0]), *loads):
        copy.start()
    for copy in loads:
        copy.wait()
    await_peers(peers)
    for n, k in enumerate(total.order):
        turn[0] = n
        if n < 7:
            for copy in block_loads(n + 1, total.order[n + 1]):
                copy.start()
        for copy in block_loads(n, k):
            copy.wait()
        if n > 1:
            for copy in results(n - 2, total.order[n - 2]):
                copy.wait()
        work(n)
        for copy in results(n, k):
            copy.start()
        total.stage(n)
        layer.stage(n)
    total.end()
    layer.end()
    for n in (6, 7):
        for copy in results(n, total.order[n]):
            copy.wait()


def ffn_second(x, dy_all, weights, hid_a, dgu_a, weights_a):
    _, rows, depth = x.shape
    width = weights.shape[1] // 3
    bf = jnp.bfloat16
    return pl.pallas_call(
        ffn_second_kernel,
        in_specs=[pl.BlockSpec(memory_space=pl.ANY)] * 6,
        out_specs=[pl.BlockSpec(memory_space=pl.ANY)] * 2
        + [pl.BlockSpec(memory_space=pltpu.VMEM)] * 2,
        out_shape=[
            jax.ShapeDtypeStruct((8, rows, width), bf),
            jax.ShapeDtypeStruct((8, rows, 2 * width), bf),
            jax.ShapeDtypeStruct((rows, depth), jnp.float32),
            jax.ShapeDtypeStruct((rows, depth), jnp.float32),
        ],
        scratch_shapes=[
            pltpu.VMEM((2, rows, depth), bf),
            pltpu.VMEM((2, rows, depth), bf),
            pltpu.VMEM((3, depth, width), bf),
            pltpu.VMEM((depth, 3 * width), bf),
            pltpu.VMEM((2, rows, width), bf),
            pltpu.VMEM((2, rows, 2 * width), bf),
            pltpu.VMEM((2, rows, width), bf),
            pltpu.VMEM((2, 2, rows, width), bf),
            pltpu.VMEM((7, rows, depth), bf),
            pltpu.VMEM((7, rows, depth), bf),
            pltpu.VMEM((7, rows, depth), bf),
            pltpu.VMEM((7, rows, depth), bf),
            pltpu.SemaphoreType.DMA((7,)),
            pltpu.SemaphoreType.DMA((7,)),
            pltpu.SemaphoreType.DMA((7,)),
            pltpu.SemaphoreType.DMA((7,)),
            pltpu.SemaphoreType.DMA((4,)),
            pltpu.SemaphoreType.DMA((4, 2)),
            pltpu.SemaphoreType.DMA((3, 2)),
        ],
        compiler_params=pltpu.CompilerParams(
            collective_id=4, has_side_effects=True, vmem_limit_bytes=VMEM_BYTES
        ),
        name="ffn_second",
    )(x, dy_all, weights, hid_a, dgu_a, weights_a)


class PlaneSum:
    def __init__(self, me, product, out_ref, to_buf, from_buf, sems):
        self.first, self.second, sibling, one, two = corner_route(me)
        self.product, self.out_ref = product, out_ref
        self.to_buf, self.from_buf = to_buf, from_buf

        def copy(i, peer):
            return lambda: remote(to_buf.at[i], from_buf.at[i], sems, i, peer)

        self.given = [copy(i, sibling) for i in range(4)]
        self.corner, self.to_one, self.to_two = copy(4, one), copy(5, one), copy(6, two)
        self.order = (7, 6, self.second + 1, self.first, self.first + 1, self.second, 1, 0)

    def give(self, k, i):
        def write(at, value):
            self.to_buf[i, :, at] = to_bf(value)

        self.product(k, write)
        self.given[i]().start()

    def pass_on(self, k, i, o, move, extra=None):
        def write(at, value):
            value = value + to_f32(self.from_buf[i, :, at])
            if extra is not None:
                value = value + to_f32(self.from_buf[extra, :, at])
            self.to_buf[o, :, at] = to_bf(value)

        self.given[i]().wait_recv()
        self.product(k, write)
        move().start()

    def stage(self, number):
        if number == 0:
            self.give(7, 0)
        elif number == 1:
            self.pass_on(6, 0, 4, self.corner)
        elif number == 2:
            self.give(self.second + 1, 1)
        elif number == 3:
            self.pass_on(self.first, 1, 5, self.to_one)
        elif number == 4:
            self.give(self.first + 1, 2)
        elif number == 5:
            self.corner().wait_recv()
            self.pass_on(self.second, 2, 6, self.to_two, 4)
        elif number == 6:
            self.give(1, 3)
        else:

            def keep(at, value):
                self.out_ref[:, at] = value

            self.product(0, keep)

    def end(self):
        self.given[3]().wait_recv()
        self.to_one().wait_recv()
        self.to_two().wait_recv()

        @pl.loop(0, self.out_ref.shape[1] // 256)
        def _(j):
            at = pl.ds(pl.multiple_of(j * 256, 256), 256)
            self.out_ref[:, at] += (
                to_f32(self.from_buf[3, :, at])
                + to_f32(self.from_buf[5, :, at])
                + to_f32(self.from_buf[6, :, at])
            )

        for move in (*self.given, self.corner, self.to_one, self.to_two):
            move().wait_send()


def column_tiles(count, body):
    @pl.loop(0, count)
    def _(j):
        body(pl.ds(pl.multiple_of(j * 256, 256), 256))


def product_sum_kernel(offsets, depths, *refs):
    count = len(depths)
    lefts, rights = refs[:count], refs[count : 2 * count]
    out_ref, left_buf, right_buf, to_buf, from_buf, send, recv, load_sem, left_sem = refs[
        2 * count :
    ]
    me = lax.axis_index("rep")
    peers = [flipped(me, k) for k in (1, 2, 4)]
    starts = [sum(depths[:i]) for i in range(len(depths))]
    call_peers(peers)
    right_loads = [
        pltpu.make_async_copy(
            rights[i].at[:, pl.ds(offsets[i], depths[i])],
            right_buf.at[:, pl.ds(starts[i], depths[i])],
            load_sem.at[i],
        )
        for i in range(count)
    ]
    for copy in right_loads:
        copy.start()

    def load(k, i):
        return pltpu.make_async_copy(
            lefts[i].at[k], left_buf.at[k, :, pl.ds(starts[i], depths[i])], left_sem.at[k, i]
        )

    def product(k, write):
        for i in range(count):
            load(k, i).wait()
        column_tiles(
            right_buf.shape[0] // 256,
            lambda at: write(at, contract_last(left_buf[k], right_buf[at, :])),
        )

    total = PlaneSum(me, product, out_ref, to_buf, from_buf, (send, recv))
    for k in total.order:
        for i in range(count):
            load(k, i).start()
    await_peers(peers)
    for copy in right_loads:
        copy.wait()
    for number in range(8):
        total.stage(number)
    total.end()


def product_sum(lefts, rights, offsets, number):
    depths = [left.shape[2] for left in lefts]
    rows = lefts[0].shape[1]
    wide = rights[0].shape[0]
    return pl.pallas_call(
        functools.partial(product_sum_kernel, offsets, depths),
        in_specs=[pl.BlockSpec(memory_space=pl.ANY)] * (2 * len(lefts)),
        out_specs=pl.BlockSpec(memory_space=pltpu.VMEM),
        out_shape=jax.ShapeDtypeStruct((rows, wide), jnp.float32),
        scratch_shapes=[
            pltpu.VMEM((8, rows, sum(depths)), jnp.bfloat16),
            pltpu.VMEM((wide, sum(depths)), jnp.bfloat16),
            pltpu.VMEM((7, rows, wide), jnp.bfloat16),
            pltpu.VMEM((7, rows, wide), jnp.bfloat16),
            pltpu.SemaphoreType.DMA((7,)),
            pltpu.SemaphoreType.DMA((7,)),
            pltpu.SemaphoreType.DMA((len(lefts),)),
            pltpu.SemaphoreType.DMA((8, len(lefts))),
        ],
        compiler_params=pltpu.CompilerParams(
            collective_id=number, has_side_effects=True, vmem_limit_bytes=VMEM_BYTES
        ),
        name=f"product_sum_{number}",
    )(*lefts, *rights)


def on_plane_of_8(
    tokens,
    cotangent,
    segment_ids,
    positions,
    projection_weight,
    projection_first_moment,
    projection_second_moment,
    out_weight,
    out_first,
    out_second,
    gate_up_weight,
    gate_up_first,
    gate_up_second,
    down_weight,
    down_first,
    down_second,
    norm_gains,
    gains_first,
    gains_second,
):
    shard_count = lax.axis_size("shard")
    shard_pos = lax.axis_index("shard")
    me = lax.axis_index("rep")
    token_rows = tokens.shape[0]
    group_rows = segment_ids.shape[0]
    plane_rows = 8 * token_rows
    owned = norm_gains.shape[1]
    q_width = QUERY_HEADS * HEAD_SIZE // 8

    def flat(parts):
        return parts.reshape(plane_rows, -1)

    def line_gather(parts):
        return lax.all_gather(flat_rows(parts), "shard", axis=0, tiled=True)

    def flat_rows(parts):
        return parts.reshape(8 * owned, -1)

    def line_sum(grad):
        return lax.psum_scatter(to_bf(grad), "shard", scatter_dimension=0, tiled=True)

    gains_b = to_f32(to_bf(norm_gains))
    turns = [gains_b] + [
        lax.ppermute(gains_b, "shard", [(i, (i - d) % shard_count) for i in range(shard_count)])
        for d in range(1, shard_count)
    ]
    gains_line = jnp.take(
        jnp.stack(turns), (jnp.arange(shard_count) - shard_pos) % shard_count, axis=0
    )
    gains_size = shard_count * 2 * owned
    notes = jnp.concatenate([gains_line.reshape(-1), to_f32(segment_ids)])
    cos_own, sin_own = tables(positions)
    angles = HEAD_SIZE // 2
    table_own = jnp.concatenate([cos_own[:, :angles], sin_own[:, :angles]], axis=1)
    table_own = jnp.pad(table_own, ((0, 0), (0, 128 - 2 * angles)))
    notes = jnp.pad(notes, (0, -notes.shape[0] % 1024)).reshape(8, -1)

    first_parts = swap_first(projection_weight, out_weight.T)
    first_w = line_gather(first_parts)
    ffn_parts = swap_ffn(after(gate_up_weight, first_parts), down_weight.T)
    ffn_a = line_gather(ffn_parts[0])
    tokens_all, notes_all, table = plane_gather(
        [after(tokens, ffn_parts[0]), notes, table_own], (None,) * 3, 9
    )
    notes_all = notes_all.reshape(8, -1)
    gain_full = (
        jnp.take(notes_all[:, :gains_size], jnp.arange(8) ^ me, axis=0)
        .reshape(8, shard_count, 2, owned)
        .transpose(2, 1, 0, 3)
        .reshape(2, MODEL_WIDTH)
    )
    gain_one = gain_full[0]
    gain_two = gain_full[1]
    seg_k = notes_all[:, gains_size : gains_size + group_rows]
    seg_q = lax.dynamic_slice_in_dim(seg_k, shard_pos * token_rows, token_rows, 1)

    normed_one, query_b, kv_own = project(tokens_all, first_w, gain_one[None, :], table)
    normed_one = flat(normed_one)
    ffn_b = line_gather(after(ffn_parts[1], tokens_all))
    out_slots, cotangent_all, kv_line = gather_keys(
        first_w, (q_width + 2 * HEAD_SIZE, q_width), cotangent, kv_own, shard_count, 10
    )
    seg_q_column, seg_k_row = seg_q[:, :, None], seg_k[:, None, :]
    seg_q_row, seg_k_column = seg_q[:, None, :], seg_k[:, :, None]
    out_b, logs, out_own = attend(query_b, kv_line, seg_q_column, seg_k_row)
    tokens_f = to_f32(tokens)
    hidden_one = tokens_f + contract_last(out_own, out_slots)
    scale_two = rms_scale(hidden_one)
    normed_two_own = to_bf(hidden_one * scale_two * gain_two)
    normed_two, hid_a, dgu_a = ffn_first(normed_two_own, cotangent_all, ffn_a)
    grad_a = ffn_gradient(normed_two, cotangent_all, dgu_a, hid_a)
    sum_a = line_sum(grad_a)
    x_late, seg_k_column, log_rows, _ = lax.optimization_barrier(
        (normed_two, seg_k_column, logs.transpose(0, 2, 1), grad_a)
    )
    hid_b, dgu_b, grad_normed_two, layer_sum = ffn_second(
        x_late, cotangent_all, ffn_b, hid_a, dgu_a, ffn_a
    )
    grad_hidden_one = to_f32(cotangent) + norm_back(
        hidden_one, scale_two, gain_two, grad_normed_two
    )
    grad_attn = to_bf(grad_hidden_one)
    grad_b = ffn_gradient(normed_two, cotangent_all, dgu_b, hid_b)
    sum_b = line_sum(grad_b)
    grad_q, grad_kv_line, grad_attn_all = attend_back(
        after(to_bf(dot(grad_attn, out_slots)), sum_a, grad_b),
        grad_attn,
        query_b,
        kv_line,
        seg_q_row,
        seg_k_column,
        log_rows,
        table,
    )
    layer_out = to_bf(hidden_one + layer_sum)
    grad_out = to_bf(outer_rows(flat(grad_attn_all), out_b))
    grad_first = jnp.concatenate([to_bf(outer_rows(normed_one, grad_q)), grad_out], axis=1)
    half = FF // 2

    def ffn_layout(at):
        return ((0, 0, 512, 0, at), (0, 512, 512, 0, FF + at), (0, 1024, 512, 1, at))

    sizes = (2 * FF, FF)
    grads_a = swap_back([after(sum_a, grad_first)], ffn_layout(0), sizes, 13)
    grad_kv = lax.psum_scatter(
        after(grad_kv_line, sum_b, *grads_a), "shard", scatter_dimension=0
    )
    grad_gu_w, grad_down_w = swap_back([sum_b], ffn_layout(half), sizes, 15, grads_a)
    grad_kv = after(grad_kv, grad_gu_w)
    sum_first = line_sum(after(grad_first, grad_kv))
    grad_gu_w = to_f32(grad_gu_w)
    grad_down_w = to_f32(grad_down_w).T
    new_gu = adamw(gate_up_weight, gate_up_first, gate_up_second, grad_gu_w, RATES[2], DECAYS[2])
    new_down = adamw(down_weight, down_first, down_second, grad_down_w, RATES[3], DECAYS[3])
    grad_kv = to_f32(grad_kv)
    angle_rows = flat(table)
    cos_table = jnp.concatenate([angle_rows[:, :angles]] * 2, axis=1)
    sin_table = jnp.concatenate([angle_rows[:, angles : 2 * angles]] * 2, axis=1)
    grad_kv_b = to_bf(
        jnp.concatenate(
            [rotate(grad_kv[:, :HEAD_SIZE], cos_table, sin_table, -1.0), grad_kv[:, HEAD_SIZE:]],
            axis=1,
        )
    )
    grad_kv_proj = to_bf(outer_rows(normed_one, grad_kv_b))
    sum_kv = line_sum(grad_kv_proj)
    grad_normed_one = product_sum(
        [
            after(grad_q, grad_kv_proj).reshape(8, token_rows, -1),
            grad_kv_b.reshape(8, token_rows, -1),
        ],
        [first_w, first_w],
        (0, q_width),
        6,
    )
    back_one = norm_back(tokens_f, rms_scale(tokens_f), gain_one, grad_normed_one)
    tokens_grad = to_bf(grad_hidden_one + back_one)

    grad_q_w, grad_kv_w, grad_out_w = swap_back(
        [sum_first, sum_kv],
        ((0, 0, 256, 0, 0), (1, 0, 128, 1, 0), (0, 256, 256, 2, 0)),
        (8 * q_width, 8 * 128, 8 * q_width),
        14,
    )
    grad_kv_w = grad_kv_w.reshape(owned, 8, 2, HEAD_SIZE).transpose(0, 2, 1, 3)
    grad_qkv_w = to_f32(jnp.concatenate([grad_q_w, grad_kv_w.reshape(owned, -1)], axis=1))
    grad_out_w = to_f32(grad_out_w).T
    grad_gain_w = (
        jnp.stack(
            [
                jnp.sum(to_f32(to_bf(projection_weight)) * grad_qkv_w, axis=1),
                jnp.sum(to_f32(to_bf(gate_up_weight)) * grad_gu_w, axis=1),
            ]
        )
        / gains_b
    )
    new_qkv = adamw(
        projection_weight,
        projection_first_moment,
        projection_second_moment,
        grad_qkv_w,
        RATES[0],
        DECAYS[0],
    )
    new_out = adamw(out_weight, out_first, out_second, grad_out_w, RATES[1], DECAYS[1])
    new_gain = adamw(norm_gains, gains_first, gains_second, grad_gain_w, RATES[4], DECAYS[4])
    return (layer_out, tokens_grad, *new_qkv, *new_out, *new_gu, *new_down, *new_gain)


def any_gather(block):
    return lax.all_gather(block, "rep", axis=0, tiled=True)


def any_sum(blocks):
    return to_f32(lax.psum_scatter(to_bf(blocks), "rep", scatter_dimension=0, tiled=True))


def any_swap(blocks):
    return lax.all_to_all(blocks, "rep", 0, 0, tiled=True)


def on_any_mesh(
    tokens,
    cotangent,
    segment_ids,
    positions,
    projection_weight,
    projection_first_moment,
    projection_second_moment,
    out_weight,
    out_first,
    out_second,
    gate_up_weight,
    gate_up_first,
    gate_up_second,
    down_weight,
    down_first,
    down_second,
    norm_gains,
    gains_first,
    gains_second,
):
    shard_count = lax.axis_size("shard")
    rep_count = lax.axis_size("rep")
    shard_pos = lax.axis_index("shard")
    token_rows = tokens.shape[0]
    group_rows = segment_ids.shape[0]
    plane_rows = rep_count * token_rows
    owned = norm_gains.shape[1]
    q_all = QUERY_HEADS * HEAD_SIZE
    kv_all = KEY_VALUE_HEADS * HEAD_SIZE
    sharers = max(1, rep_count // KEY_VALUE_HEADS)
    kv_heads = max(1, KEY_VALUE_HEADS // rep_count)
    q_heads = QUERY_HEADS // rep_count
    q_each = q_heads // kv_heads
    q_width = q_heads * HEAD_SIZE
    kv_width = kv_heads * HEAD_SIZE
    ff_width = FF // rep_count
    score_scale = HEAD_SIZE ** (-0.5)

    def pieces(rows, width):
        return to_bf(rows).reshape(owned, -1, width).transpose(1, 0, 2)

    def kv_pieces(rows):
        return jnp.repeat(pieces(rows, kv_width), sharers, axis=0)

    def whole(parts):
        mine = any_swap(parts).reshape(rep_count * owned, -1)
        return lax.all_gather(mine, "shard", axis=0, tiled=True)

    proj = whole(
        jnp.concatenate(
            [
                pieces(projection_weight[:, :q_all], q_width),
                kv_pieces(projection_weight[:, q_all : q_all + kv_all]),
                kv_pieces(projection_weight[:, q_all + kv_all :]),
            ],
            axis=2,
        )
    )
    out_w = whole(pieces(out_weight.T, q_width))
    gate_w = whole(pieces(gate_up_weight[:, :FF], ff_width))
    up_w = whole(pieces(gate_up_weight[:, FF:], ff_width))
    down_w = whole(pieces(down_weight.T, ff_width))

    gains_b = to_f32(to_bf(norm_gains))
    gains_line = lax.all_gather(gains_b, "shard", axis=0)
    notes = jnp.concatenate(
        [gains_line.reshape(-1), to_f32(positions), to_f32(segment_ids)]
    ).reshape(1, -1)
    notes_all = any_gather(notes)
    gains_size = shard_count * 2 * owned
    gain_full = (
        notes_all[:, :gains_size]
        .reshape(rep_count, shard_count, 2, owned)
        .transpose(2, 1, 0, 3)
        .reshape(2, MODEL_WIDTH)
    )
    gain_one = gain_full[0]
    gain_two = gain_full[1]
    plane_pos = notes_all[:, gains_size : gains_size + token_rows].reshape(plane_rows)
    plane_seg = notes_all[:, gains_size + token_rows :]

    tokens_all = to_f32(any_gather(tokens))
    normed_one = to_bf(tokens_all * rms_scale(tokens_all) * gain_one)
    qkv = dot(normed_one, proj)
    cos_table, sin_table = tables(plane_pos)
    query_b = to_bf(rotate(qkv[:, :q_width], cos_table, sin_table, 1.0))
    key_b = to_bf(rotate(qkv[:, q_width : q_width + kv_width], cos_table, sin_table, 1.0))
    value_b = to_bf(qkv[:, q_width + kv_width :])
    kv_line = lax.all_gather(jnp.concatenate([key_b, value_b], axis=1), "shard", axis=0)
    kv_groups = (
        kv_line.reshape(shard_count, rep_count, token_rows, 2 * kv_width)
        .transpose(1, 0, 2, 3)
        .reshape(rep_count, group_rows, 2, kv_heads, HEAD_SIZE)
    )
    key_groups = kv_groups[:, :, 0].transpose(0, 2, 1, 3)
    value_groups = kv_groups[:, :, 1].transpose(0, 2, 1, 3)

    def to_heads(flat):
        return flat.reshape(rep_count, token_rows, kv_heads, q_each, HEAD_SIZE).transpose(
            0, 2, 3, 1, 4
        )

    def from_heads(heads):
        return heads.transpose(0, 3, 1, 2, 4).reshape(plane_rows, q_width)

    query_heads = to_heads(query_b)
    row_at = shard_pos * token_rows + jnp.arange(token_rows, dtype=jnp.int32)
    causal = jnp.arange(group_rows, dtype=jnp.int32)[None, :] <= row_at[:, None]

    def masked_scores(q_one, k_one, seg_one):
        seg_rows = lax.dynamic_slice_in_dim(seg_one, shard_pos * token_rows, token_rows, 0)
        allowed = (seg_rows[:, None] == seg_one[None, :]) & causal
        scores = (
            jnp.einsum("hgqd,hkd->hgqk", q_one, k_one, preferred_element_type=jnp.float32)
            * score_scale
        )
        return jnp.where(allowed[None, None], scores, -1e30)

    def group_forward(packed):
        q_one, k_one, v_one, seg_one = packed
        scores = masked_scores(q_one, k_one, seg_one)
        peak_score = jnp.max(scores, axis=-1, keepdims=True)
        exp_total = jnp.sum(jnp.exp(scores - peak_score), axis=-1, keepdims=True)
        log_sum = peak_score + jnp.log(exp_total)
        probs = to_bf(jnp.exp(scores - log_sum))
        attended = jnp.einsum("hgqk,hkd->hgqd", probs, v_one, preferred_element_type=jnp.float32)
        return (to_bf(attended), log_sum)

    attended, log_sums = lax.map(
        group_forward, (query_heads, key_groups, value_groups, plane_seg)
    )
    out_b = from_heads(attended)
    tokens_f = to_f32(tokens)
    hidden_one = tokens_f + any_sum(contract_last(out_b, out_w))
    scale_two = rms_scale(hidden_one)
    normed_two = any_gather(to_bf(hidden_one * scale_two * gain_two))
    gate_part = dot(normed_two, gate_w)
    up_part = dot(normed_two, up_w)
    sigmoid_gate = jax.nn.sigmoid(gate_part)
    silu_gate = gate_part * sigmoid_gate
    hidden_b = to_bf(silu_gate * up_part)
    layer_out = to_bf(hidden_one + any_sum(contract_last(hidden_b, down_w)))

    cotangent_all = any_gather(cotangent)
    grad_hidden = dot(cotangent_all, down_w)
    grad_gate_b = to_bf(
        grad_hidden * up_part * sigmoid_gate * (1.0 + gate_part * (1.0 - sigmoid_gate))
    )
    grad_up_b = to_bf(grad_hidden * silu_gate)
    grad_normed_two = any_sum(
        contract_last(grad_gate_b, gate_w) + contract_last(grad_up_b, up_w)
    )
    grad_hidden_one = to_f32(cotangent) + norm_back(
        hidden_one, scale_two, gain_two, grad_normed_two
    )
    grad_attn_b = any_gather(to_bf(grad_hidden_one))
    out_grad_heads = to_heads(to_bf(dot(grad_attn_b, out_w)))

    def group_backward(packed):
        q_one, k_one, v_one, seg_one, d_one, log_sum = packed
        probs = jnp.exp(masked_scores(q_one, k_one, seg_one) - log_sum)
        grad_probs = jnp.einsum("hgqd,hkd->hgqk", d_one, v_one, preferred_element_type=jnp.float32)
        inner = jnp.sum(grad_probs * probs, axis=-1, keepdims=True)
        grad_scores = to_bf(probs * (grad_probs - inner))
        grad_q = (
            jnp.einsum("hgqk,hkd->hgqd", grad_scores, k_one, preferred_element_type=jnp.float32)
            * score_scale
        )
        grad_k = (
            jnp.einsum("hgqk,hgqd->khd", grad_scores, q_one, preferred_element_type=jnp.float32)
            * score_scale
        )
        grad_v = jnp.einsum(
            "hgqk,hgqd->khd", to_bf(probs), d_one, preferred_element_type=jnp.float32
        )
        both = jnp.stack([grad_k, grad_v], axis=1).reshape(group_rows, 2 * kv_width)
        return (grad_q, to_bf(both))

    grad_q, grad_kv = lax.map(
        group_backward,
        (query_heads, key_groups, value_groups, plane_seg, out_grad_heads, log_sums),
    )
    grad_kv = (
        grad_kv.reshape(rep_count, shard_count, token_rows, 2 * kv_width)
        .transpose(1, 0, 2, 3)
        .reshape(shard_count * plane_rows, 2 * kv_width)
    )
    grad_kv = to_f32(lax.psum_scatter(grad_kv, "shard", scatter_dimension=0, tiled=True))
    grad_qkv_b = to_bf(
        jnp.concatenate(
            [
                rotate(from_heads(grad_q), cos_table, sin_table, -1.0),
                rotate(grad_kv[:, :kv_width], cos_table, sin_table, -1.0),
                grad_kv[:, kv_width:],
            ],
            axis=1,
        )
    )
    grad_normed_one = any_sum(contract_last(grad_qkv_b, proj))
    back_one = norm_back(tokens_f, rms_scale(tokens_f), gain_one, grad_normed_one)
    tokens_grad = to_bf(grad_hidden_one + back_one)

    def owner_pieces(grad):
        summed = lax.psum_scatter(to_bf(grad), "shard", scatter_dimension=0, tiled=True)
        return to_f32(any_swap(summed.reshape(rep_count, owned, -1)))

    def row_of(parts):
        return parts.transpose(1, 0, 2).reshape(owned, -1)

    def kv_row_of(parts):
        return row_of(parts.reshape(-1, sharers, owned, kv_width).sum(axis=1))

    down_parts = owner_pieces(outer_rows(cotangent_all, hidden_b))
    gate_parts = owner_pieces(outer_rows(normed_two, grad_gate_b))
    up_parts = owner_pieces(outer_rows(normed_two, grad_up_b))
    out_parts = owner_pieces(outer_rows(grad_attn_b, out_b))
    proj_parts = owner_pieces(outer_rows(normed_one, grad_qkv_b))
    grad_down_w = row_of(down_parts).T
    grad_gu_w = jnp.concatenate([row_of(gate_parts), row_of(up_parts)], axis=1)
    grad_out_w = row_of(out_parts).T
    grad_qkv_w = jnp.concatenate(
        [
            row_of(proj_parts[..., :q_width]),
            kv_row_of(proj_parts[..., q_width : q_width + kv_width]),
            kv_row_of(proj_parts[..., q_width + kv_width :]),
        ],
        axis=1,
    )
    grad_gain_w = (
        jnp.stack(
            [
                jnp.sum(to_f32(to_bf(projection_weight)) * grad_qkv_w, axis=1),
                jnp.sum(to_f32(to_bf(gate_up_weight)) * grad_gu_w, axis=1),
            ]
        )
        / gains_b
    )
    new_qkv = adamw(
        projection_weight,
        projection_first_moment,
        projection_second_moment,
        grad_qkv_w,
        RATES[0],
        DECAYS[0],
    )
    new_out = adamw(out_weight, out_first, out_second, grad_out_w, RATES[1], DECAYS[1])
    new_gu = adamw(gate_up_weight, gate_up_first, gate_up_second, grad_gu_w, RATES[2], DECAYS[2])
    new_down = adamw(down_weight, down_first, down_second, grad_down_w, RATES[3], DECAYS[3])
    new_gain = adamw(norm_gains, gains_first, gains_second, grad_gain_w, RATES[4], DECAYS[4])
    return (layer_out, tokens_grad, *new_qkv, *new_out, *new_gu, *new_down, *new_gain)


def solution(mesh):
    rows = P(("rep", "shard"), None)
    wide = P(("shard", "rep"), None)
    tall = P(None, ("shard", "rep"))
    in_specs = (
        (rows, rows, P("rep"), P(("rep", "shard")))
        + (wide,) * 3
        + (tall,) * 3
        + (wide,) * 3
        + (tall,) * 6
    )
    out_specs = (rows, rows) + (wide,) * 3 + (tall,) * 3 + (wide,) * 3 + (tall,) * 6
    on_device = on_plane_of_8 if mesh.shape["rep"] == 8 else on_any_mesh
    return jax.shard_map(
        on_device, mesh=mesh, in_specs=in_specs, out_specs=out_specs, check_vma=False
    )
```
